256 devices in a mesh: expert: 64 (over y, z, core), half: 4 (over x).
Axes of the slice: x: 4, y: 4, z: 8, core: 2. Of those that a mesh axis runs over, the one named last changes fastest.
Arguments:
- tokens: bfloat16 [16384, 2048], P('expert', 'half'), may hold values from -6 to 6
- out_grad: bfloat16 [16384, 2048], P('expert', 'half'), may hold values from -6 to 6
- w_gate: bfloat16 [128, 768, 2048], P('expert', 'half'), may hold values from -0.125 to 0.125
- w_up: bfloat16 [128, 768, 2048], P('expert', 'half'), may hold values from -0.125 to 0.125
- w_down: bfloat16 [128, 768, 2048], P('expert', 'half'), may hold values from -0.21875 to 0.21875
- chosen_rows: int32 [128, 64, 8], P(None, 'expert'), may hold values from 0 to 255, as said below
- counts: int32 [128, 64], P(None, 'expert'), may hold values from 1 to 8, 256 in all within a row
- gate_values: bfloat16 [128, 64, 8], P(None, 'expert'), may hold values from 0.099609375 to 1
Outputs:
- grad_tokens: bfloat16 [16384, 2048], P('expert', 'half')
- grad_w_gate: bfloat16 [128, 768, 2048], P('expert', 'half')
- grad_w_up: bfloat16 [128, 768, 2048], P('expert', 'half')
- grad_w_down: bfloat16 [128, 768, 2048], P('expert', 'half')
- gate_grad: bfloat16 [128, 64, 8], P(None, 'expert')
The draws below stay inside these ranges and needn't reach their ends.
Inputs may be any that keep to these rules, and one draw needn't show every extreme that they name: `chosen_rows`: for each expert and token group the first counts entries are distinct positions in the group of 256 tokens; entries past counts are positions too and are unused. For each expert the counts over all token groups sum to 256.
All inputs are finite; a program needn't handle non-finite values.
Results may differ from the reference program's by a relative error of at most 0.017.
Values may be sent and summed in bfloat16 or wider, within the bound.
A program may use at most 128 MiB of HBM per device.

```python
import math
import jax
import jax.numpy as jnp
import numpy as np
from jax import lax

D = 2048
FF = 768
TOK_DEV = 256
MOST = 8
SOURCES = 64
EXPERTS = 128
TOKENS = 16384
CAP = 256


def draw_chosen_rows(key, part):
    scores = jax.random.randint(key, (EXPERTS, SOURCES, TOK_DEV), 0, 1 << 20, dtype=jnp.int32)
    scores = scores * TOK_DEV + jnp.arange(TOK_DEV, dtype=jnp.int32)[None, None, :]
    order = jnp.argsort(scores, axis=-1, stable=True)
    return order[:, :, :MOST].astype(jnp.int32)


def level_of(key, shape, shards, low, top_value):
    gain = 1.0
    for axis_at, parts in shards:
        heights = jax.random.uniform(jax.random.fold_in(jax.random.fold_in(key, 6), axis_at), (parts,), jnp.float32, low / len(shards), top_value / len(shards))
        gain = gain * jnp.repeat(jnp.exp(heights), shape[axis_at] // parts).reshape((-1,) + (1,) * (len(shape) - 1 - axis_at))
    return gain


def profile(amount, total, most, slope):
    loads = [(1 << 20) // math.isqrt(standing ** slope) + 1 for standing in range(2, amount + 1)]
    rest, holding = total - most - (amount - 1), [1] * (amount - 1)
    while rest > 0:
        free = [i for i in range(amount - 1) if holding[i] < most]
        pool, left = sum([loads[i] for i in free]), rest
        for i in free:
            extra = min(most - holding[i], max(1, left * loads[i] // pool), rest)
            holding[i] = holding[i] + extra
            rest = rest - extra
    return np.array([most] + holding)


def ragged(stream_key, amount, total, limit, lean):
    if amount == 2:
        one = jax.random.randint(stream_key, (), max(1, total - limit), min(limit, total - 1) + 1)
        return jnp.stack([one, total - one])
    lengths = jnp.asarray(profile(amount, total, limit, lean), jnp.int32)
    couples = (amount - 1) // 2
    donor, receiver = lengths[1:1 + 2 * couples:2], lengths[2:2 + 2 * couples:2]
    room = jnp.minimum(donor - 1, limit - receiver)
    shifted = jax.random.randint(jax.random.fold_in(stream_key, 1), (couples,), 0, 1 << 20) % (room + 1)
    lengths = lengths.at[1:1 + 2 * couples:2].set(donor - shifted).at[2:2 + 2 * couples:2].set(receiver + shifted)
    return lengths[jax.random.permutation(jax.random.fold_in(stream_key, 2), amount)]


def bell_draw(stream_key, extent, scale, limit, split=(), held_as=jnp.bfloat16):
    values = jax.random.normal(stream_key, extent, jnp.float32) * scale
    if len(split) > 0:
        values = level_of(stream_key, extent, split, -0.22, 0.18) * values
    return jnp.clip(values, min=-limit, max=limit).astype(held_as)


def setup_inputs(seed: int = 0) -> dict:
    seeds = jax.random.split(jax.random.key(seed), 9)
    return {
        "tokens": bell_draw(seeds[0], (TOKENS, D), 1.0, 6.0, ((0, 64), (1, 4))),
        "out_grad": bell_draw(seeds[1], (TOKENS, D), 1.0, 6.0, ((0, 64), (1, 4))),
        "w_gate": bell_draw(seeds[2], (EXPERTS, FF, D), D ** -0.5, 0.125, ((0, 64), (1, 4))),
        "w_up": bell_draw(seeds[3], (EXPERTS, FF, D), D ** -0.5, 0.125, ((0, 64), (1, 4))),
        "w_down": bell_draw(seeds[4], (EXPERTS, FF, D), FF ** -0.5, 0.21875, ((0, 64), (1, 4))),
        "chosen_rows": draw_chosen_rows(jax.random.fold_in(seeds[8], 71), 0),
        "counts": jax.vmap(lambda own: ragged(own, SOURCES, CAP, MOST, 2))(jax.random.split(seeds[6], EXPERTS)).reshape((EXPERTS, SOURCES)).astype(jnp.int32),
        "gate_values": jnp.clip(jnp.exp(math.log(1.0) - 2.306499 * jax.random.uniform(seeds[7], (EXPERTS, SOURCES, MOST), jnp.float32) ** level_of(seeds[7], (EXPERTS, SOURCES, MOST), ((1, 64),), -0.2, 0.2)), 0.099609375, 1.0).astype(jnp.bfloat16),
    }


def reference(tokens, out_grad, w_gate, w_up, w_down, chosen_rows, counts, gate_values):
    def expert_pass(accum_rows, inputs):
        rows_e, counts_e, gates_e, weight_gate, weight_up, weight_down = inputs
        row_base = (jnp.arange(SOURCES, dtype=jnp.int32) * TOK_DEV)[:, None]
        row_index = (row_base + rows_e).reshape(-1).astype(jnp.int32)
        live_slots = (jnp.arange(MOST, dtype=jnp.int32)[None, :] < counts_e[:, None]).reshape(-1)
        gate_live = jnp.where(live_slots, gates_e.reshape(-1), jnp.zeros((), gates_e.dtype))
        x_rows = jnp.take(tokens, row_index, axis=0)
        dy_rows = jnp.take(out_grad, row_index, axis=0)
        pre_gate = jnp.dot(x_rows, weight_gate.T, preferred_element_type=jnp.float32)
        pre_up = jnp.dot(x_rows, weight_up.T, preferred_element_type=jnp.float32)
        back_proj = jnp.dot(dy_rows, weight_down.T, preferred_element_type=jnp.float32)
        sigmoid_gate = jax.nn.sigmoid(pre_gate)
        activated = pre_gate * sigmoid_gate
        hidden = (activated * pre_up).astype(jnp.bfloat16)
        gate_wide = gate_live.astype(jnp.float32)[:, None]
        scaled = (gate_wide * dy_rows.astype(jnp.float32)).astype(jnp.bfloat16)
        slot_sums = jnp.sum(hidden.astype(jnp.float32) * back_proj, axis=1)
        gate_grad = jnp.where(live_slots, slot_sums, jnp.zeros((), slot_sums.dtype)).astype(jnp.bfloat16)
        d_hidden = gate_wide * back_proj
        d_gate = (d_hidden * pre_up * sigmoid_gate * (1.0 + pre_gate * (1.0 - sigmoid_gate))).astype(jnp.bfloat16)
        d_up = (d_hidden * activated).astype(jnp.bfloat16)
        grad_down = jnp.dot(hidden.T, scaled, preferred_element_type=jnp.float32).astype(jnp.bfloat16)
        grad_gate = jnp.dot(d_gate.T, x_rows, preferred_element_type=jnp.float32).astype(jnp.bfloat16)
        grad_up = jnp.dot(d_up.T, x_rows, preferred_element_type=jnp.float32).astype(jnp.bfloat16)
        row_grad = (jnp.dot(d_gate, weight_gate, preferred_element_type=jnp.float32)
                    + jnp.dot(d_up, weight_up, preferred_element_type=jnp.float32)).astype(jnp.bfloat16)
        accum_rows = accum_rows.at[row_index].add(row_grad.astype(jnp.float32))
        return accum_rows, (grad_gate, grad_up, grad_down, gate_grad.reshape(SOURCES, MOST))

    start_rows = jnp.zeros((TOKENS, D), jnp.float32)
    summed, outputs = lax.scan(expert_pass, start_rows,
                               (chosen_rows, counts, gate_values, w_gate, w_up, w_down))
    grad_w_gate, grad_w_up, grad_w_down, gate_grad = outputs
    return summed.astype(jnp.bfloat16), grad_w_gate, grad_w_up, grad_w_down, gate_grad
```

```python
import functools

import jax
import jax.numpy as jnp
from jax import lax
from jax.experimental import pallas as pl
from jax.experimental.pallas import tpu as pltpu
from jax.sharding import PartitionSpec as P

MESH = pl.DeviceIdType.MESH
F32, BF16 = jnp.float32, jnp.bfloat16


def iota(shape, dim):
    return lax.broadcasted_iota(jnp.int32, shape, dim)


def dot(a, b, dims=((1,), (0,)), precision=None):
    return lax.dot_general(a, b, (dims, ((), ())), preferred_element_type=F32, precision=precision)


def kernel(
    n_src, n_half,
    tok, out_grad, chosen, counts, gates, wg_hbm, wu_hbm, wd_hbm,
    gt_out, gwg_out, gwu_out, gwd_out, gg_out,
    w_buf, w_sem,
    cnt_send, cnt_recv, fwd_send, fwd_recv,
    home_g, pack, spread,
    rows_all, part_send, part_recv, part_own,
    gg_part, gg_recv, ggh_send, ggh_recv,
    ret_send, ret_recv, grads, grad_sem,
    cnt_ss, cnt_rs, fwd_ss, fwd_rs, ag_ss, ag_rs, rs_ss, rs_rs,
    ggx_ss, ggx_rs, ret_ss, ret_rs, ggh_ss, ggh_rs,
):
    me = lax.axis_index("expert")
    half = lax.axis_index("half")
    tokens = tok.shape[0]
    quarter = tok.shape[1]
    fold = quarter // 2
    slots = n_src * 16
    cap = rows_all.shape[3]
    hid = wg_hbm.shape[1]

    barrier = pltpu.get_barrier_semaphore()

    @pl.loop(1, n_src)
    def _(i):
        pl.semaphore_signal(barrier, inc=1, device_id={"expert": lax.rem(me + i, n_src)}, device_id_type=MESH)

    for i in range(1, n_half):
        pl.semaphore_signal(barrier, inc=1, device_id={"half": lax.rem(half + i, n_half)}, device_id_type=MESH)

    loads = [
        pltpu.make_async_copy(ref, w_buf.at[k], w_sem.at[k]) for k, ref in enumerate((wg_hbm, wu_hbm, wd_hbm))
    ]
    for load in loads:
        load.start()

    experts, most = chosen.shape
    live = iota((experts, most), 1) < counts[...]
    chosen_live = jnp.where(live, chosen[...], -1).astype(F32).astype(BF16)
    gates_live = jnp.where(live, gates[...].astype(F32), 0.0).astype(BF16)

    count_wide = jnp.broadcast_to(counts[...].astype(F32), (experts, 128)).astype(BF16)
    lane = iota((n_src, 128), 1)
    rows_to = jnp.zeros((n_src, 128), F32)
    for e in range(2):
        pick = (iota((n_src, experts), 1) == 2 * iota((n_src, experts), 0) + e).astype(BF16)
        rows_to = rows_to + jnp.where(lane == e, dot(pick, count_wide), 0.0)
    cnt_send[...] = rows_to.reshape(n_src, 1, 128)

    def send_all(src, dst, ss, rs):
        @pl.loop(1, n_src)
        def _(i):
            to = lax.rem(me + i, n_src)
            pltpu.make_async_remote_copy(
                src_ref=src.at[to], dst_ref=dst.at[me], send_sem=ss, recv_sem=rs,
                device_id={"expert": to}, device_id_type=MESH,
            ).start()

    def wait_all(buf, sem):
        part = buf.at[pl.ds(0, n_src - 1)]
        pltpu.make_async_copy(part, part, sem).wait()

    low = (iota((slots, fold), 0) // 8) % 2 == 0
    col_pick = [
        (iota((slots, experts), 1) == 2 * (iota((slots, experts), 0) // 16) + e).astype(BF16) for e in range(2)
    ]
    slot_j = iota((slots, most), 1) == iota((slots, most), 0) % 8
    ones = jnp.ones((most, tokens), BF16)

    def spread_column(e, table):
        picked = jnp.where(slot_j, dot(col_pick[e], table), 0.0).astype(BF16)
        return dot(picked, ones)

    def folded(wide):
        return jnp.where(low, wide[:, :fold], wide[:, fold:])

    hot = [spread_column(e, chosen_live) == iota((slots, tokens), 1).astype(F32) for e in range(2)]

    def fill(k, picker, src):
        block = folded(dot(picker, src[...])).astype(BF16).reshape(n_src, 16, fold)
        fwd_send[k] = block

    fill(0, hot[0].astype(BF16), tok)
    pl.semaphore_wait(barrier, n_src - 1 + n_half - 1)
    send_all(cnt_send, cnt_recv, cnt_ss, cnt_rs)
    send_all(fwd_send.at[0], fwd_recv.at[0], fwd_ss.at[0], fwd_rs.at[0])
    fill(1, hot[1].astype(BF16), tok)
    send_all(fwd_send.at[1], fwd_recv.at[1], fwd_ss.at[1], fwd_rs.at[1])
    for e in range(2):
        fill(2 + e, jnp.where(hot[e], spread_column(e, gates_live), 0.0).astype(BF16), out_grad)
        send_all(fwd_send.at[2 + e], fwd_recv.at[2 + e], fwd_ss.at[2 + e], fwd_rs.at[2 + e])
    cnt_recv[me] = cnt_send[me]
    for k in range(4):
        fwd_recv[k, me] = fwd_send[k, me]

    wide_chosen = dot(chosen_live, (iota((most, slots), 0) == iota((most, slots), 1) % 8).astype(BF16))
    in_fold = (iota((tokens, slots), 1) // 8) % 2
    for e in range(2):
        mine = iota((experts, slots), 0) == 2 * (iota((experts, slots), 1) // 16) + e
        row = jnp.sum(jnp.where(mine, wide_chosen, 0.0), axis=0, keepdims=True)
        hit = row == iota((tokens, slots), 0).astype(F32)
        for f in range(2):
            home_g[e, f] = jnp.where(hit & (in_fold == f), 1.0, 0.0).astype(BF16)

    wait_all(cnt_recv, cnt_rs)
    count_all = cnt_recv[...].reshape(n_src, 128).astype(BF16)
    for e in range(2):
        by_col = dot(count_all, (iota((128, slots), 0) == e).astype(BF16))
        src_of = iota((n_src, slots), 1) // 16
        before = jnp.sum(jnp.where(iota((n_src, slots), 0) < src_of, by_col, 0.0), axis=0, keepdims=True)
        size = jnp.sum(jnp.where(iota((n_src, slots), 0) == src_of, by_col, 0.0), axis=0, keepdims=True)
        j = (iota((1, slots), 1) % 8).astype(F32)
        place = jnp.where(j < size, before + j, -1.0)
        hit = place == iota((cap, slots), 0).astype(F32)
        in_fold_r = (iota((cap, slots), 1) // 8) % 2
        for f in range(2):
            pack[e, f] = jnp.where(hit & (in_fold_r == f), 1.0, 0.0).astype(BF16)
        own_wide = dot(count_all, (iota((128, cap), 0) == e).astype(BF16)).astype(BF16)
        src_row = iota((slots, n_src), 0) // 16
        before_c = dot((iota((slots, n_src), 1) < src_row).astype(BF16), own_wide)
        size_c = dot((iota((slots, n_src), 1) == src_row).astype(BF16), own_wide)
        j_c = (iota((slots, cap), 0) % 8).astype(F32)
        place_c = jnp.where(j_c < size_c, before_c + j_c, -1.0)
        spread[e] = jnp.where(place_c == iota((slots, cap), 1).astype(F32), 1.0, 0.0).astype(BF16)

    def gather_copies(a, e):
        k = 2 * a + e
        return [
            pltpu.make_async_remote_copy(
                src_ref=rows_all.at[a, e, half], dst_ref=rows_all.at[a, e, half],
                send_sem=ag_ss.at[k], recv_sem=ag_rs.at[k],
                device_id={"half": lax.rem(half + i, n_half)}, device_id_type=MESH,
            )
            for i in (2, 1, 3)
        ]

    def take_in(a, e):
        k = 2 * a + e
        wait_all(fwd_recv.at[k], fwd_rs.at[k])
        got = fwd_recv[k].reshape(slots, fold)
        for f in range(2):
            rows_all[a, e, half, :, pl.ds(f * fold, fold)] = dot(pack[e, f], got).astype(BF16)
        for copy in gather_copies(a, e):
            copy.start()

    def wait_gather(a, e):
        part = rows_all.at[a, e, pl.ds(0, n_half - 1)]
        pltpu.make_async_copy(part, part, ag_rs.at[2 * a + e]).wait()

    def project(w, a, e):
        total = jnp.zeros((hid, cap), F32)
        for h in range(n_half):
            total = total + dot(
                w_buf[w, e, :, pl.ds(h * quarter, quarter)], rows_all[a, e, h], ((1,), (1,))
            )
        return total

    def compute(e):
        wait_gather(0, e)
        pre_gate = project(0, 0, e)
        pre_up = project(1, 0, e)
        wait_gather(1, e)
        back = project(2, 1, e)
        sig = 1.0 / (1.0 + jnp.exp(-pre_gate))
        act = pre_gate * sig
        hidden = (act * pre_up).astype(BF16)
        d_gate = (back * pre_up * sig * (1.0 + pre_gate * (1.0 - sig))).astype(BF16)
        d_up = (back * act).astype(BF16)
        dg_r = jnp.transpose(d_gate)
        du_r = jnp.transpose(d_up)
        for i in (2, 1, 3, 0):
            to = lax.rem(half + i, n_half)
            cols = pl.ds(pl.multiple_of(to * quarter, quarter), quarter)
            value = dot(dg_r, w_buf[0, e, :, cols]) + dot(du_r, w_buf[1, e, :, cols])
            if i == 0:
                part_own[e] = value
            else:
                part_send[e, i - 1] = value.astype(BF16)
                pltpu.make_async_remote_copy(
                    src_ref=part_send.at[e, i - 1], dst_ref=part_recv.at[e, i - 1],
                    send_sem=rs_ss.at[e], recv_sem=rs_rs.at[e],
                    device_id={"half": to}, device_id_type=MESH,
                ).start()
        gg = jnp.sum(hidden.astype(F32) * back, axis=0, keepdims=True)
        gg_part[e] = jnp.broadcast_to(gg, (8, cap))
        for i in range(1, n_half):
            pltpu.make_async_remote_copy(
                src_ref=gg_part.at[e], dst_ref=gg_recv.at[e, i - 1],
                send_sem=ggx_ss.at[e], recv_sem=ggx_rs.at[e],
                device_id={"half": lax.rem(half + i, n_half)}, device_id_type=MESH,
            ).start()
        return hidden, d_gate, d_up

    def weight_grads(e, hidden, d_gate, d_up):
        for h in range(n_half):
            cols = pl.ds(h * quarter, quarter)
            x_h = rows_all[0, e, h]
            grads[0, e, :, cols] = dot(d_gate, x_h).astype(BF16)
            grads[1, e, :, cols] = dot(d_up, x_h).astype(BF16)
            grads[2, e, :, cols] = dot(hidden, rows_all[1, e, h]).astype(BF16)

    def send_home(e):
        pltpu.make_async_copy(part_send.at[e], part_recv.at[e], rs_rs.at[e]).wait()
        total = part_own[e]
        for i in range(n_half - 1):
            total = total + part_recv[e, i].astype(F32)
        block = folded(dot(spread[e], total.astype(BF16))).astype(BF16)
        ret_send[e] = block.reshape(n_src, 16, fold)
        send_all(ret_send.at[e], ret_recv.at[e], ret_ss.at[e], ret_rs.at[e])
        ret_recv[e, me] = ret_send[e, me]

    def gate_home():
        total = jnp.zeros((n_src, 128), F32)
        for e in range(2):
            pltpu.make_async_copy(gg_recv.at[e], gg_recv.at[e], ggx_rs.at[e]).wait()
            gg = gg_part[e]
            for i in range(n_half - 1):
                gg = gg + gg_recv[e, i]
            top = gg.astype(BF16).astype(F32)
            mid = (gg - top).astype(BF16).astype(F32)
            rest = gg - top - mid
            sub = iota((8, cap), 0)
            split = jnp.where(sub == 0, top, jnp.where(sub == 1, mid, jnp.where(sub == 2, rest, 0.0)))
            row = jnp.sum(dot(split.astype(BF16), pack[e, 0]), axis=0, keepdims=True)
            own = iota((n_src, slots), 1) // 16 == iota((n_src, slots), 0)
            spread_row = jnp.where(own, jnp.broadcast_to(row, (n_src, slots)), 0.0)
            col = iota((slots, 128), 0)
            to_lane = ((col // 8) % 2 == 0) & (iota((slots, 128), 1) == e * 8 + col % 8)
            total = total + dot(spread_row, to_lane.astype(F32), precision=lax.Precision.HIGHEST)
        ggh_send[...] = total.reshape(n_src, 1, 128)
        send_all(ggh_send, ggh_recv, ggh_ss, ggh_rs)
        ggh_recv[me] = ggh_send[me]

    take_in(0, 0)
    take_in(0, 1)
    take_in(1, 0)
    take_in(1, 1)
    for load in loads:
        load.wait()
    state0 = compute(0)
    state1 = compute(1)
    send_home(0)
    gate_home()
    weight_grads(0, *state0)
    send_home(1)
    weight_grads(1, *state1)
    stores = [
        pltpu.make_async_copy(grads.at[k], ref, grad_sem.at[k])
        for k, ref in enumerate((gwg_out, gwu_out, gwd_out))
    ]
    for store in stores:
        store.start()

    wait_all(ggh_recv, ggh_rs)
    got = ggh_recv[...].reshape(n_src, 128)
    gg_rows = jnp.zeros((experts, most), F32)
    for e in range(2):
        lanes = (iota((128, most), 0) == e * 8 + iota((128, most), 1)).astype(F32)
        place = (iota((experts, n_src), 0) == 2 * iota((experts, n_src), 1) + e).astype(F32)
        picked = dot(got, lanes, precision=lax.Precision.HIGHEST)
        gg_rows = gg_rows + dot(place, picked, precision=lax.Precision.HIGHEST)
    gg_out[...] = jnp.where(live, gg_rows / gates[...].astype(F32), 0.0).astype(BF16)

    wait_all(ret_recv.at[0], ret_rs.at[0])
    first = [dot(home_g[0, f], ret_recv[0].reshape(slots, fold)) for f in range(2)]
    wait_all(ret_recv.at[1], ret_rs.at[1])
    for f in range(2):
        last = first[f] + dot(home_g[1, f], ret_recv[1].reshape(slots, fold))
        gt_out[:, pl.ds(f * fold, fold)] = last.astype(BF16)

    wait_all(cnt_send, cnt_ss)
    wait_all(ggh_send, ggh_ss)
    for k in range(4):
        wait_all(fwd_send.at[k], fwd_ss.at[k])
    for a in range(2):
        for e in range(2):
            part = rows_all.at[a, e, pl.ds(0, n_half - 1)]
            pltpu.make_async_copy(part, part, ag_ss.at[2 * a + e]).wait()
    for e in range(2):
        pltpu.make_async_copy(part_send.at[e], part_send.at[e], rs_ss.at[e]).wait()
        pltpu.make_async_copy(gg_recv.at[e], gg_recv.at[e], ggx_ss.at[e]).wait()
        wait_all(ret_send.at[e], ret_ss.at[e])
    for store in stores:
        store.wait()


def body(n_src, n_half, tokens, out_grad, w_gate, w_up, w_down, chosen_rows, counts, gate_values):
    tok_dev, quarter = tokens.shape
    experts, _, most = chosen_rows.shape
    per, hid, width = w_gate.shape
    cap = 4 * n_src
    fold = quarter // 2
    vmem = pl.BlockSpec(memory_space=pltpu.VMEM)
    hbm = pl.BlockSpec(memory_space=pl.ANY)
    dma = pltpu.SemaphoreType.DMA
    grad_w = jax.ShapeDtypeStruct(w_gate.shape, BF16)
    outs = pl.pallas_call(
        functools.partial(kernel, n_src, n_half),
        out_shape=(
            jax.ShapeDtypeStruct(tokens.shape, BF16),
            grad_w, grad_w, grad_w,
            jax.ShapeDtypeStruct((experts, most), BF16),
        ),
        in_specs=[vmem] * 5 + [hbm] * 3,
        out_specs=(vmem, hbm, hbm, hbm, vmem),
        scratch_shapes=[
            pltpu.VMEM((3, per, hid, width), BF16),
            dma((3,)),
            pltpu.VMEM((n_src, 1, 128), F32),
            pltpu.VMEM((n_src, 1, 128), F32),
            pltpu.VMEM((4, n_src, 16, fold), BF16),
            pltpu.VMEM((4, n_src, 16, fold), BF16),
            pltpu.VMEM((2, 2, tok_dev, n_src * 16), BF16),
            pltpu.VMEM((2, 2, cap, n_src * 16), BF16),
            pltpu.VMEM((2, n_src * 16, cap), BF16),
            pltpu.VMEM((2, 2, n_half, cap, quarter), BF16),
            pltpu.VMEM((2, n_half - 1, cap, quarter), BF16),
            pltpu.VMEM((2, n_half - 1, cap, quarter), BF16),
            pltpu.VMEM((2, cap, quarter), F32),
            pltpu.VMEM((2, 8, cap), F32),
            pltpu.VMEM((2, n_half - 1, 8, cap), F32),
            pltpu.VMEM((n_src, 1, 128), F32),
            pltpu.VMEM((n_src, 1, 128), F32),
            pltpu.VMEM((2, n_src, 16, fold), BF16),
            pltpu.VMEM((2, n_src, 16, fold), BF16),
            pltpu.VMEM((3, per, hid, width), BF16),
            dma((3,)),
            dma, dma, dma((4,)), dma((4,)), dma((4,)), dma((4,)), dma((2,)), dma((2,)),
            dma((2,)), dma((2,)), dma((2,)), dma((2,)), dma, dma,
        ],
        compiler_params=pltpu.CompilerParams(
            collective_id=0, has_side_effects=True, vmem_limit_bytes=56 * 2**20
        ),
        cost_estimate=pl.CostEstimate(flops=4 * 10**9, bytes_accessed=10**7, transcendentals=10**5),
        name="experts_backward",
    )(
        tokens, out_grad,
        chosen_rows.reshape(experts, most), counts, gate_values.reshape(experts, most),
        w_gate, w_up, w_down,
    )
    return outs[:4] + (outs[4].reshape(experts, 1, most),)


def solution(mesh):
    return jax.shard_map(
        functools.partial(body, mesh.shape["expert"], mesh.shape["half"]),
        mesh=mesh,
        in_specs=(
            P("expert", "half"),
            P("expert", "half"),
            P("expert", "half", None),
            P("expert", "half", None),
            P("expert", "half", None),
            P(None, "expert", None),
            P(None, "expert"),
            P(None, "expert", None),
        ),
        out_specs=(
            P("expert", "half"),
            P("expert", "half", None),
            P("expert", "half", None),
            P("expert", "half", None),
            P(None, "expert", None),
        ),
        check_vma=False,
    )
```

```python
import functools

import jax
import jax.numpy as jnp
from jax import lax
from jax.experimental import pallas as pl
from jax.experimental.pallas import tpu as pltpu
from jax.sharding import PartitionSpec as P

MESH = pl.DeviceIdType.MESH
F32, BF16 = jnp.float32, jnp.bfloat16
NT = ((1,), (1,))
PIECES = tuple((a, e, q) for e in range(2) for a in range(2) for q in range(2))


def iota(shape, dim):
    return lax.broadcasted_iota(jnp.int32, shape, dim)


def dot(a, b, dims=((1,), (0,)), precision=None):
    return lax.dot_general(a, b, (dims, ((), ())), preferred_element_type=F32, precision=precision)


def kernel(
    n_src, n_half,
    tok_hbm, out_grad_hbm, chosen_hbm, counts_hbm, gates_hbm, wg_hbm, wu_hbm, wd_hbm,
    gt_out, grads_g, grads_u, grads_d, gg_out,
    tok, out_grad, chosen, counts, gates, in_sem,
    w_buf, w_sem, hot_buf,
    cnt_send, cnt_recv, fwd_send, fwd_recv,
    home_g, pack, spread,
    rows_all, part_send, part_recv, part_own, keep,
    gg_part, gg_recv, ggh_send, ggh_recv,
    ret_send, ret_recv,
    cnt_ss, cnt_rs, fwd_ss, fwd_rs, ag_ss, ag_rs, rs_ss, rs_rs,
    ggx_ss, ggx_rs, ret_ss, ret_rs, ggh_ss, ggh_rs,
):
    me = lax.axis_index("expert")
    half = lax.axis_index("half")
    tokens = tok.shape[0]
    quarter = tok.shape[1]
    fold = quarter // 2
    lane = fold // 2
    slots = n_src * 16
    cap = rows_all.shape[4]
    mid = cap // 2
    hid = wg_hbm.shape[1]
    most, experts = chosen.shape
    piece_of = {piece: k for k, piece in enumerate(PIECES)}

    ins = [
        pltpu.make_async_copy(src, dst, in_sem.at[k])
        for k, (src, dst) in enumerate((
            (chosen_hbm, chosen), (counts_hbm, counts), (gates_hbm, gates), (tok_hbm, tok), (out_grad_hbm, out_grad)
        ))
    ]
    loads = [
        pltpu.make_async_copy(ref, w_buf.at[k], w_sem.at[k]) for k, ref in enumerate((wg_hbm, wu_hbm, wd_hbm))
    ]
    for copy in ins:
        copy.start()

    barrier = pltpu.get_barrier_semaphore()

    @pl.loop(1, n_src)
    def _(i):
        pl.semaphore_signal(barrier, inc=1, device_id={"expert": lax.rem(me + i, n_src)}, device_id_type=MESH)

    for i in range(1, n_half):
        pl.semaphore_signal(barrier, inc=1, device_id={"half": lax.rem(half + i, n_half)}, device_id_type=MESH)

    for copy in ins:
        copy.wait()
    for load in loads:
        load.start()

    live = iota((most, experts), 0) < counts[...]
    chosen_live = jnp.where(live, chosen[...], -1).astype(F32).astype(BF16)
    gates_live = jnp.where(live, gates[...].astype(F32), 0.0).astype(BF16)

    def send_all(src, dst, ss, rs):
        @pl.loop(1, n_src)
        def _(i):
            to = lax.rem(me + i, n_src)
            pltpu.make_async_remote_copy(
                src_ref=src.at[to], dst_ref=dst.at[me], send_sem=ss, recv_sem=rs,
                device_id={"expert": to}, device_id_type=MESH,
            ).start()

    def wait_for(buf, sem):
        pltpu.make_async_copy(buf, buf, sem).wait()

    def wait_all(buf, sem):
        wait_for(buf.at[pl.ds(0, n_src - 1)], sem)

    def folded(wide):
        low = (iota((slots, lane), 0) // 8) % 2 == 0
        return jnp.where(low, wide[:, :lane], wide[:, lane:]).astype(BF16).reshape(n_src, 16, lane)

    def spread_column(e, table):
        mine = (iota((slots, experts), 1) == 2 * (iota((slots, experts), 0) // 16) + e).astype(BF16)
        slot_j = iota((slots, most), 1) == iota((slots, most), 0) % 8
        picked = jnp.where(slot_j, dot(mine, table, NT), 0.0).astype(BF16)
        return dot(picked, jnp.ones((most, tokens), BF16))

    def pick(a, e):
        hot = spread_column(e, chosen_live) == iota((slots, tokens), 1).astype(F32)
        value = 1.0 if a == 0 else spread_column(e, gates_live)
        hot_buf[...] = jnp.where(hot, value, 0.0).astype(BF16)

    def fill(a, e, q):
        k = piece_of[a, e, q]
        src = tok if a == 0 else out_grad
        fwd_send[k] = folded(dot(hot_buf[...], src[:, pl.ds(q * fold, fold)]))
        fwd_recv[k, me] = fwd_send[k, me]

    def send_piece(k):
        send_all(fwd_send.at[k], fwd_recv.at[k], fwd_ss.at[k], fwd_rs.at[k])

    pick(0, 0)
    fill(0, 0, 0)
    pl.semaphore_wait(barrier, n_src - 1 + n_half - 1)
    send_piece(0)
    count_wide = jnp.broadcast_to(counts[...].astype(F32), (128, experts)).astype(BF16)
    rows_to = jnp.zeros((n_src, 128), F32)
    for e in range(2):
        mine = (iota((n_src, experts), 1) == 2 * iota((n_src, experts), 0) + e).astype(BF16)
        rows_to = rows_to + jnp.where(iota((n_src, 128), 1) == e, dot(mine, count_wide, NT), 0.0)
    cnt_send[...] = rows_to.reshape(n_src, 1, 128)
    cnt_recv[me] = cnt_send[me]
    send_all(cnt_send, cnt_recv, cnt_ss, cnt_rs)
    fill(0, 0, 1)
    send_piece(1)
    pick(1, 0)
    fill(1, 0, 0)
    send_piece(2)
    fill(1, 0, 1)
    send_piece(3)

    def make_pack(e):
        count_all = cnt_recv[...].reshape(n_src, 128).astype(BF16)
        by_col = dot(count_all, (iota((128, slots), 0) == e).astype(BF16))
        src_of = iota((n_src, slots), 1) // 16
        before = jnp.sum(jnp.where(iota((n_src, slots), 0) < src_of, by_col, 0.0), axis=0, keepdims=True)
        size = jnp.sum(jnp.where(iota((n_src, slots), 0) == src_of, by_col, 0.0), axis=0, keepdims=True)
        j = (iota((1, slots), 1) % 8).astype(F32)
        place = jnp.where(j < size, before + j, -1.0)
        hit = place == iota((cap, slots), 0).astype(F32)
        in_half = (iota((cap, slots), 1) // 8) % 2
        for g in range(2):
            pack[e, g] = jnp.where(hit & (in_half == g), 1.0, 0.0).astype(BF16)

    def make_spread(e):
        count_all = cnt_recv[...].reshape(n_src, 128).astype(BF16)
        own_wide = dot(count_all, (iota((128, cap), 0) == e).astype(BF16)).astype(BF16)
        src_row = iota((slots, n_src), 0) // 16
        before = dot((iota((slots, n_src), 1) < src_row).astype(BF16), own_wide)
        size = dot((iota((slots, n_src), 1) == src_row).astype(BF16), own_wide)
        j = (iota((slots, cap), 0) % 8).astype(F32)
        place = jnp.where(j < size, before + j, -1.0)
        spread[e] = jnp.where(place == iota((slots, cap), 1).astype(F32), 1.0, 0.0).astype(BF16)

    def make_home(e):
        in_half = (iota((tokens, slots), 1) // 8) % 2
        mine = (iota((experts, slots), 0) == 2 * (iota((experts, slots), 1) // 16) + e).astype(BF16)
        row = dot(chosen_live, mine)
        row = jnp.sum(jnp.where(iota((most, slots), 0) == iota((most, slots), 1) % 8, row, 0.0), axis=0, keepdims=True)
        hit = row == iota((tokens, slots), 0).astype(F32)
        for g in range(2):
            home_g[e, g] = jnp.where(hit & (in_half == g), 1.0, 0.0).astype(BF16)

    def to_half(src, dst, ss, rs, step):
        return pltpu.make_async_remote_copy(
            src_ref=src, dst_ref=dst, send_sem=ss, recv_sem=rs,
            device_id={"half": lax.rem(half + step, n_half)}, device_id_type=MESH,
        )

    low_rows, high_rows = pl.ds(0, mid), pl.ds(mid, mid)

    def take_in(a, e, q):
        k = piece_of[a, e, q]

        def pass_on(ref, n, step):
            to_half(ref, ref, ag_ss.at[k, n], ag_rs.at[k, n], step).start()

        wait_all(fwd_recv.at[k], fwd_rs.at[k])
        got = fwd_recv[k].reshape(slots, lane)
        for g in range(2):
            rows_all[a, e, q, half, :, pl.ds(g * lane, lane)] = dot(pack[e, g], got).astype(BF16)
        mine = rows_all.at[a, e, q, half]
        pass_on(mine.at[low_rows], 0, 1)
        pass_on(mine.at[high_rows], 1, 3)
        pass_on(mine.at[high_rows], 2, 1)
        pass_on(mine.at[low_rows], 3, 3)
        left = rows_all.at[a, e, q, lax.rem(half + 3, n_half), low_rows]
        right = rows_all.at[a, e, q, lax.rem(half + 1, n_half), high_rows]
        wait_for(left, ag_rs.at[k, 0])
        pass_on(left, 4, 1)
        wait_for(right, ag_rs.at[k, 1])
        pass_on(right, 5, 3)

    def wait_gather(a, e):
        for q in range(2):
            for n in (2, 3, 4, 5):
                wait_for(rows_all.at[a, e, q, 0, low_rows], ag_rs.at[piece_of[a, e, q], n])

    def project(w, a, e):
        total = jnp.zeros((hid, cap), F32)
        for h in range(n_half):
            for q in range(2):
                cols = pl.ds(h * quarter + q * fold, fold)
                total = total + dot(w_buf[w, e, :, cols], rows_all[a, e, q, h], NT)
        return total

    def forward(e):
        wait_gather(0, e)
        pre_gate = project(0, 0, e)
        pre_up = project(1, 0, e)
        sig = 1.0 / (1.0 + jnp.exp(-pre_gate))
        act = pre_gate * sig
        hidden = (act * pre_up).astype(BF16)
        slope = pre_up * sig * (1.0 + pre_gate * (1.0 - sig))
        return hidden, act, slope

    def backward(e, hidden, act, slope):
        wait_gather(1, e)
        back = project(2, 1, e)
        d_gate = (back * slope).astype(BF16)
        d_up = (back * act).astype(BF16)
        dg_r = jnp.transpose(d_gate)
        du_r = jnp.transpose(d_up)
        for q in range(2):
            s = 2 * e + q

            def value(step):
                to = lax.rem(half + step, n_half)
                cols = pl.ds(pl.multiple_of(to * quarter + q * fold, fold), fold)
                return dot(dg_r, w_buf[0, e, :, cols]) + dot(du_r, w_buf[1, e, :, cols])

            def push(n, block, step):
                part_send[s, n] = block.astype(BF16)
                to_half(part_send.at[s, n], part_recv.at[s, n], rs_ss.at[s, n], rs_rs.at[s, n], step).start()

            far = value(2)
            push(0, far[:mid], 1)
            push(1, far[mid:], 3)
            right = value(1)
            push(2, right[mid:], 1)
            keep[s, 0] = right[:mid]
            left = value(3)
            push(3, left[:mid], 3)
            keep[s, 1] = left[mid:]
            part_own[s] = value(0)
        gg = jnp.sum(hidden.astype(F32) * back, axis=0, keepdims=True)
        gg_part[e] = jnp.broadcast_to(gg, (8, cap))
        for i in range(1, n_half):
            to_half(gg_part.at[e], gg_recv.at[e, i - 1], ggx_ss.at[e], ggx_rs.at[e], i).start()
        return d_gate, d_up

    def relay(e):
        for q in range(2):
            s = 2 * e + q
            for n, step in ((0, 1), (1, 3)):
                wait_for(part_recv.at[s, n], rs_rs.at[s, n])
                part_send[s, 4 + n] = (keep[s, n] + part_recv[s, n].astype(F32)).astype(BF16)
                to_half(
                    part_send.at[s, 4 + n], part_recv.at[s, 4 + n], rs_ss.at[s, 4 + n], rs_rs.at[s, 4 + n], step
                ).start()

    def weight_grads(e, hidden, d_gate, d_up):
        for h in range(n_half):
            for q in range(2):
                cols = pl.ds(h * quarter + q * fold, fold)
                x_h = rows_all[0, e, q, h]
                grads_g[e, :, cols] = dot(d_gate, x_h).astype(BF16)
                grads_u[e, :, cols] = dot(d_up, x_h).astype(BF16)
                grads_d[e, :, cols] = dot(hidden, rows_all[1, e, q, h]).astype(BF16)

    def send_home(e, q):
        s = 2 * e + q
        for n in (2, 3, 4, 5):
            wait_for(part_recv.at[s, n], rs_rs.at[s, n])
        low = part_own[s, low_rows] + part_recv[s, 4].astype(F32) + part_recv[s, 3].astype(F32)
        high = part_own[s, high_rows] + part_recv[s, 2].astype(F32) + part_recv[s, 5].astype(F32)
        total = jnp.concatenate([low.astype(BF16), high.astype(BF16)], axis=0)
        ret_send[s] = folded(dot(spread[e], total))
        ret_recv[s, me] = ret_send[s, me]
        send_all(ret_send.at[s], ret_recv.at[s], ret_ss.at[s], ret_rs.at[s])

    def gate_home():
        total = jnp.zeros((n_src, 128), F32)
        for e in range(2):
            wait_for(gg_recv.at[e], ggx_rs.at[e])
            gg = gg_part[e]
            for i in range(n_half - 1):
                gg = gg + gg_recv[e, i]
            top = gg.astype(BF16).astype(F32)
            mid_part = (gg - top).astype(BF16).astype(F32)
            rest = gg - top - mid_part
            sub = iota((8, cap), 0)
            split = jnp.where(sub == 0, top, jnp.where(sub == 1, mid_part, jnp.where(sub == 2, rest, 0.0)))
            row = jnp.sum(dot(split.astype(BF16), pack[e, 0]), axis=0, keepdims=True)
            own = iota((n_src, slots), 1) // 16 == iota((n_src, slots), 0)
            spread_row = jnp.where(own, jnp.broadcast_to(row, (n_src, slots)), 0.0)
            col = iota((slots, 128), 0)
            to_lane = ((col // 8) % 2 == 0) & (iota((slots, 128), 1) == e * 8 + col % 8)
            total = total + dot(spread_row, to_lane.astype(F32), precision=lax.Precision.HIGHEST)
        ggh_send[...] = total.reshape(n_src, 1, 128)
        ggh_recv[me] = ggh_send[me]
        send_all(ggh_send, ggh_recv, ggh_ss, ggh_rs)

    wait_all(cnt_recv, cnt_rs)
    make_pack(0)
    take_in(*PIECES[0])
    pick(0, 1)
    fill(0, 1, 0)
    send_piece(4)
    take_in(*PIECES[1])
    fill(0, 1, 1)
    send_piece(5)
    for load in loads:
        load.wait()
    take_in(*PIECES[2])
    pick(1, 1)
    fill(1, 1, 0)
    send_piece(6)
    fwd0 = forward(0)
    take_in(*PIECES[3])
    fill(1, 1, 1)
    send_piece(7)
    make_pack(1)
    take_in(*PIECES[4])
    back0 = backward(0, *fwd0)
    make_spread(0)
    take_in(*PIECES[5])
    relay(0)
    make_spread(1)
    take_in(*PIECES[6])
    fwd1 = forward(1)
    make_home(0)
    take_in(*PIECES[7])
    send_home(0, 0)
    send_home(0, 1)
    back1 = backward(1, *fwd1)
    weight_grads(0, fwd0[0], *back0)
    relay(1)
    gate_home()
    make_home(1)
    send_home(1, 0)
    send_home(1, 1)
    weight_grads(1, fwd1[0], *back1)

    wait_all(ggh_recv, ggh_rs)
    got = ggh_recv[...].reshape(n_src, 128)
    gg_rows = jnp.zeros((most, experts), F32)
    for e in range(2):
        lanes = (iota((most, 128), 1) == e * 8 + iota((most, 128), 0)).astype(F32)
        place = (iota((n_src, experts), 1) == 2 * iota((n_src, experts), 0) + e).astype(F32)
        picked = dot(lanes, got, NT, precision=lax.Precision.HIGHEST)
        gg_rows = gg_rows + dot(picked, place, precision=lax.Precision.HIGHEST)
    gg_out[...] = jnp.where(live, gg_rows / gates[...].astype(F32), 0.0).astype(BF16)

    def home_sum(s):
        wait_all(ret_recv.at[s], ret_rs.at[s])
        got = ret_recv[s].reshape(slots, lane)
        return [dot(home_g[s // 2, g], got) for g in range(2)]

    first = [home_sum(0), home_sum(1)]
    for q in range(2):
        last = home_sum(2 + q)
        for g in range(2):
            gt_out[:, pl.ds(q * fold + g * lane, lane)] = (first[q][g] + last[g]).astype(BF16)

    wait_all(cnt_send, cnt_ss)
    wait_all(ggh_send, ggh_ss)
    for k, (a, e, q) in enumerate(PIECES):
        wait_all(fwd_send.at[k], fwd_ss.at[k])
        for n in range(6):
            wait_for(rows_all.at[a, e, q, 0, low_rows], ag_ss.at[k, n])
    for s in range(4):
        wait_all(ret_send.at[s], ret_ss.at[s])
        for n in range(6):
            wait_for(part_send.at[s, n], rs_ss.at[s, n])
    for e in range(2):
        wait_for(gg_recv.at[e], ggx_ss.at[e])


def write_out(a, b, c, d, e, ao, bo, co, do, eo, sem):
    copies = [
        pltpu.make_async_copy(src, dst, sem.at[k])
        for k, (src, dst) in enumerate(((b, bo), (c, co), (d, do), (a, ao), (e, eo)))
    ]
    for copy in copies:
        copy.start()
    for copy in copies:
        copy.wait()


def body(n_src, n_half, tokens, out_grad, w_gate, w_up, w_down, chosen_rows, counts, gate_values):
    tok_dev, quarter = tokens.shape
    experts, _, most = chosen_rows.shape
    per, hid, width = w_gate.shape
    cap = 4 * n_src
    fold = quarter // 2
    lane = fold // 2
    slots = n_src * 16
    vmem = pl.BlockSpec(memory_space=pltpu.VMEM)
    hbm = pl.BlockSpec(memory_space=pltpu.HBM)
    dma = pltpu.SemaphoreType.DMA
    grad_w = jax.ShapeDtypeStruct(w_gate.shape, BF16)
    shapes = (
        jax.ShapeDtypeStruct(tokens.shape, BF16),
        grad_w, grad_w, grad_w,
        jax.ShapeDtypeStruct((most, experts), BF16),
    )
    args = (
        tokens, out_grad,
        chosen_rows.reshape(experts, most).T, counts.T, gate_values.reshape(experts, most).T,
        w_gate, w_up, w_down,
    )
    outs = pl.pallas_call(
        functools.partial(kernel, n_src, n_half),
        out_shape=tuple(pltpu.VMEM(s.shape, s.dtype) for s in shapes),
        in_specs=[hbm] * 8,
        out_specs=(vmem,) * 5,
        scratch_shapes=[
            pltpu.VMEM(tokens.shape, BF16),
            pltpu.VMEM(tokens.shape, BF16),
            pltpu.VMEM((most, experts), jnp.int32),
            pltpu.VMEM((1, experts), jnp.int32),
            pltpu.VMEM((most, experts), BF16),
            dma((5,)),
            pltpu.VMEM((3, per, hid, width), BF16),
            dma((3,)),
            pltpu.VMEM((slots, tok_dev), BF16),
            pltpu.VMEM((n_src, 1, 128), F32),
            pltpu.VMEM((n_src, 1, 128), F32),
            pltpu.VMEM((8, n_src, 16, lane), BF16),
            pltpu.VMEM((8, n_src, 16, lane), BF16),
            pltpu.VMEM((2, 2, tok_dev, slots), BF16),
            pltpu.VMEM((2, 2, cap, slots), BF16),
            pltpu.VMEM((2, slots, cap), BF16),
            pltpu.VMEM((2, 2, 2, n_half, cap, fold), BF16),
            pltpu.VMEM((4, 6, cap // 2, fold), BF16),
            pltpu.VMEM((4, 6, cap // 2, fold), BF16),
            pltpu.VMEM((4, cap, fold), F32),
            pltpu.VMEM((4, 2, cap // 2, fold), F32),
            pltpu.VMEM((2, 8, cap), F32),
            pltpu.VMEM((2, n_half - 1, 8, cap), F32),
            pltpu.VMEM((n_src, 1, 128), F32),
            pltpu.VMEM((n_src, 1, 128), F32),
            pltpu.VMEM((4, n_src, 16, lane), BF16),
            pltpu.VMEM((4, n_src, 16, lane), BF16),
            dma, dma, dma((8,)), dma((8,)), dma((8, 6)), dma((8, 6)), dma((4, 6)), dma((4, 6)),
            dma((2,)), dma((2,)), dma((4,)), dma((4,)), dma, dma,
        ],
        compiler_params=pltpu.CompilerParams(
            collective_id=0, has_side_effects=True, vmem_limit_bytes=46 * 2**20
        ),
        cost_estimate=pl.CostEstimate(flops=4 * 10**9, bytes_accessed=10**7, transcendentals=10**5),
        name="experts_backward",
    )(*(pltpu.with_memory_space_constraint(a, pltpu.HBM) for a in args))
    outs = pl.pallas_call(
        write_out,
        out_shape=shapes,
        in_specs=[pl.BlockSpec(memory_space=pl.ANY)] * 5,
        out_specs=(hbm,) * 5,
        scratch_shapes=[dma((5,))],
        compiler_params=pltpu.CompilerParams(vmem_limit_bytes=2**20),
        name="write_out",
    )(*outs)
    return outs[:4] + (outs[4].T.reshape(experts, 1, most),)


def solution(mesh):
    return jax.shard_map(
        functools.partial(body, mesh.shape["expert"], mesh.shape["half"]),
        mesh=mesh,
        in_specs=(
            P("expert", "half"),
            P("expert", "half"),
            P("expert", "half", None),
            P("expert", "half", None),
            P("expert", "half", None),
            P(None, "expert", None),
            P(None, "expert"),
            P(None, "expert", None),
        ),
        out_specs=(
            P("expert", "half"),
            P("expert", "half", None),
            P("expert", "half", None),
            P("expert", "half", None),
            P(None, "expert", None),
        ),
        check_vma=False,
    )
```

```python
import functools

import jax
import jax.numpy as jnp
from jax import lax
from jax.experimental import pallas as pl
from jax.experimental.pallas import tpu as pltpu
from jax.sharding import PartitionSpec as P

MESH = pl.DeviceIdType.MESH
F32, BF16 = jnp.float32, jnp.bfloat16
NT = ((1,), (1,))
PIECES = tuple((a, e, q) for e in range(2) for a in range(2) for q in range(2))


def iota(shape, dim):
    return lax.broadcasted_iota(jnp.int32, shape, dim)


def dot(a, b, dims=((1,), (0,)), precision=None):
    return lax.dot_general(a, b, (dims, ((), ())), preferred_element_type=F32, precision=precision)


def kernel(
    n_src, n_half,
    tok_hbm, out_grad_hbm, chosen_hbm, counts_hbm, gates_hbm, wg_hbm, wu_hbm, wd_hbm,
    gt_out, grads_g, grads_u, grads_d, gg_out,
    tok, out_grad, chosen, counts, gates, in_sem,
    w_buf, w_sem, hot_buf,
    cnt_send, cnt_recv, fwd_send, fwd_recv,
    home_g, pack, spread,
    rows_all, part_send, part_recv, part_own, keep,
    gg_part, gg_recv, ggh_send, ggh_recv,
    ret_send, ret_recv,
    cnt_ss, cnt_rs, fwd_ss, fwd_rs, ag_ss, ag_rs, rs_ss, rs_rs,
    ggx_ss, ggx_rs, ret_ss, ret_rs, ggh_ss, ggh_rs,
):
    me = lax.axis_index("expert")
    half = lax.axis_index("half")
    tokens = tok.shape[0]
    quarter = tok.shape[1]
    fold = quarter // 2
    lane = fold // 2
    slots = n_src * 16
    cap = rows_all.shape[4]
    mid = cap // 2
    hid = wg_hbm.shape[1]
    most, experts = chosen.shape
    piece_of = {piece: k for k, piece in enumerate(PIECES)}

    ins = [
        pltpu.make_async_copy(src, dst, in_sem.at[k])
        for k, (src, dst) in enumerate((
            (chosen_hbm, chosen), (counts_hbm, counts), (gates_hbm, gates), (tok_hbm, tok), (out_grad_hbm, out_grad)
        ))
    ]
    loads = [
        pltpu.make_async_copy(ref, w_buf.at[k], w_sem.at[k]) for k, ref in enumerate((wg_hbm, wu_hbm, wd_hbm))
    ]
    for copy in ins:
        copy.start()

    barrier = pltpu.get_barrier_semaphore()

    @pl.loop(1, n_src)
    def _(i):
        pl.semaphore_signal(barrier, inc=1, device_id={"expert": lax.rem(me + i, n_src)}, device_id_type=MESH)

    for i in range(1, n_half):
        pl.semaphore_signal(barrier, inc=1, device_id={"half": lax.rem(half + i, n_half)}, device_id_type=MESH)

    for copy in ins:
        copy.wait()
    for load in loads:
        load.start()

    live = iota((most, experts), 0) < counts[...]
    chosen_live = jnp.where(live, chosen[...], -1).astype(F32).astype(BF16)
    gates_live = jnp.where(live, gates[...].astype(F32), 0.0).astype(BF16)

    def send_all(src, dst, ss, rs):
        @pl.loop(1, n_src)
        def _(i):
            to = lax.rem(me + i, n_src)
            pltpu.make_async_remote_copy(
                src_ref=src.at[to], dst_ref=dst.at[me], send_sem=ss, recv_sem=rs,
                device_id={"expert": to}, device_id_type=MESH,
            ).start()

    def wait_for(buf, sem):
        pltpu.make_async_copy(buf, buf, sem).wait()

    def wait_all(buf, sem):
        wait_for(buf.at[pl.ds(0, n_src - 1)], sem)

    def folded(wide):
        low = (iota((slots, lane), 0) // 8) % 2 == 0
        return jnp.where(low, wide[:, :lane], wide[:, lane:]).astype(BF16).reshape(n_src, 16, lane)

    def spread_column(e, table):
        mine = (iota((slots, experts), 1) == 2 * (iota((slots, experts), 0) // 16) + e).astype(BF16)
        slot_j = iota((slots, most), 1) == iota((slots, most), 0) % 8
        picked = jnp.where(slot_j, dot(mine, table, NT), 0.0).astype(BF16)
        return dot(picked, jnp.ones((most, tokens), BF16))

    def pick(a, e):
        hot = spread_column(e, chosen_live) == iota((slots, tokens), 1).astype(F32)
        value = 1.0 if a == 0 else spread_column(e, gates_live)
        hot_buf[...] = jnp.where(hot, value, 0.0).astype(BF16)

    def fill(a, e, q):
        k = piece_of[a, e, q]
        src = tok if a == 0 else out_grad
        fwd_send[k] = folded(dot(hot_buf[...], src[:, pl.ds(q * fold, fold)]))
        fwd_recv[k, me] = fwd_send[k, me]

    def send_piece(k):
        send_all(fwd_send.at[k], fwd_recv.at[k], fwd_ss.at[k], fwd_rs.at[k])

    ahead = 3

    def prep(k):
        if k >= len(PIECES):
            return
        a, e, q = PIECES[k]
        if q == 0:
            pick(a, e)
        fill(a, e, q)

    prep(0)
    pl.semaphore_wait(barrier, n_src - 1 + n_half - 1)
    send_piece(0)
    count_wide = jnp.broadcast_to(counts[...].astype(F32), (128, experts)).astype(BF16)
    rows_to = jnp.zeros((n_src, 128), F32)
    for e in range(2):
        mine = (iota((n_src, experts), 1) == 2 * iota((n_src, experts), 0) + e).astype(BF16)
        rows_to = rows_to + jnp.where(iota((n_src, 128), 1) == e, dot(mine, count_wide, NT), 0.0)
    cnt_send[...] = rows_to.reshape(n_src, 1, 128)
    cnt_recv[me] = cnt_send[me]
    send_all(cnt_send, cnt_recv, cnt_ss, cnt_rs)
    for k in range(1, ahead):
        prep(k)
        send_piece(k)
    prep(ahead)

    def make_pack(e):
        count_all = cnt_recv[...].reshape(n_src, 128).astype(BF16)
        by_col = dot(count_all, (iota((128, slots), 0) == e).astype(BF16))
        src_of = iota((n_src, slots), 1) // 16
        before = jnp.sum(jnp.where(iota((n_src, slots), 0) < src_of, by_col, 0.0), axis=0, keepdims=True)
        size = jnp.sum(jnp.where(iota((n_src, slots), 0) == src_of, by_col, 0.0), axis=0, keepdims=True)
        j = (iota((1, slots), 1) % 8).astype(F32)
        place = jnp.where(j < size, before + j, -1.0)
        hit = place == iota((cap, slots), 0).astype(F32)
        in_half = (iota((cap, slots), 1) // 8) % 2
        for g in range(2):
            pack[e, g] = jnp.where(hit & (in_half == g), 1.0, 0.0).astype(BF16)

    def make_spread(e):
        count_all = cnt_recv[...].reshape(n_src, 128).astype(BF16)
        own_wide = dot(count_all, (iota((128, cap), 0) == e).astype(BF16)).astype(BF16)
        src_row = iota((slots, n_src), 0) // 16
        before = dot((iota((slots, n_src), 1) < src_row).astype(BF16), own_wide)
        size = dot((iota((slots, n_src), 1) == src_row).astype(BF16), own_wide)
        j = (iota((slots, cap), 0) % 8).astype(F32)
        place = jnp.where(j < size, before + j, -1.0)
        spread[e] = jnp.where(place == iota((slots, cap), 1).astype(F32), 1.0, 0.0).astype(BF16)

    def make_home(e):
        in_half = (iota((tokens, slots), 1) // 8) % 2
        mine = (iota((experts, slots), 0) == 2 * (iota((experts, slots), 1) // 16) + e).astype(BF16)
        row = dot(chosen_live, mine)
        row = jnp.sum(jnp.where(iota((most, slots), 0) == iota((most, slots), 1) % 8, row, 0.0), axis=0, keepdims=True)
        hit = row == iota((tokens, slots), 0).astype(F32)
        for g in range(2):
            home_g[e, g] = jnp.where(hit & (in_half == g), 1.0, 0.0).astype(BF16)

    def to_half(src, dst, ss, rs, step):
        return pltpu.make_async_remote_copy(
            src_ref=src, dst_ref=dst, send_sem=ss, recv_sem=rs,
            device_id={"half": lax.rem(half + step, n_half)}, device_id_type=MESH,
        )

    low_rows, high_rows = pl.ds(0, mid), pl.ds(mid, mid)

    def take_in(a, e, q):
        k = piece_of[a, e, q]

        def pass_on(ref, n, step):
            to_half(ref, ref, ag_ss.at[k, n], ag_rs.at[k, n], step).start()

        wait_all(fwd_recv.at[k], fwd_rs.at[k])
        got = fwd_recv[k].reshape(slots, lane)
        for g in range(2):
            rows_all[a, e, q, half, :, pl.ds(g * lane, lane)] = dot(pack[e, g], got).astype(BF16)
        mine = rows_all.at[a, e, q, half]
        pass_on(mine.at[low_rows], 0, 1)
        pass_on(mine.at[high_rows], 1, 3)
        pass_on(mine.at[high_rows], 2, 1)
        pass_on(mine.at[low_rows], 3, 3)
        if k + ahead < len(PIECES):
            send_piece(k + ahead)
            prep(k + ahead + 1)
        left = rows_all.at[a, e, q, lax.rem(half + 3, n_half), low_rows]
        right = rows_all.at[a, e, q, lax.rem(half + 1, n_half), high_rows]
        wait_for(left, ag_rs.at[k, 0])
        pass_on(left, 4, 1)
        wait_for(right, ag_rs.at[k, 1])
        pass_on(right, 5, 3)

    def wait_gather(a, e):
        for q in range(2):
            for n in (2, 3, 4, 5):
                wait_for(rows_all.at[a, e, q, 0, low_rows], ag_rs.at[piece_of[a, e, q], n])

    def project(w, a, e):
        total = jnp.zeros((hid, cap), F32)
        for h in range(n_half):
            for q in range(2):
                cols = pl.ds(h * quarter + q * fold, fold)
                total = total + dot(w_buf[w, e, :, cols], rows_all[a, e, q, h], NT)
        return total

    def forward(e):
        wait_gather(0, e)
        pre_gate = project(0, 0, e)
        pre_up = project(1, 0, e)
        sig = 1.0 / (1.0 + jnp.exp(-pre_gate))
        act = pre_gate * sig
        hidden = (act * pre_up).astype(BF16)
        slope = pre_up * sig * (1.0 + pre_gate * (1.0 - sig))
        return hidden, act, slope

    def row_block(e, q, step, dg_r, du_r):
        to = lax.rem(half + step, n_half)
        cols = pl.ds(pl.multiple_of(to * quarter + q * fold, fold), fold)
        return dot(dg_r, w_buf[0, e, :, cols]) + dot(du_r, w_buf[1, e, :, cols])

    def push(s, n, block, step):
        part_send[s, n] = block.astype(BF16)
        to_half(part_send.at[s, n], part_recv.at[s, n], rs_ss.at[s, n], rs_rs.at[s, n], step).start()

    def push_far(e, q, *rows):
        s = 2 * e + q
        far = row_block(e, q, 2, *rows)
        push(s, 0, far[:mid], 1)
        push(s, 1, far[mid:], 3)

    def push_near(e, q, *rows):
        s = 2 * e + q
        right = row_block(e, q, 1, *rows)
        push(s, 2, right[mid:], 1)
        keep[s, 0] = right[:mid]
        left = row_block(e, q, 3, *rows)
        push(s, 3, left[:mid], 3)
        keep[s, 1] = left[mid:]

    def relay(e, q):
        s = 2 * e + q
        for n, step in ((0, 1), (1, 3)):
            wait_for(part_recv.at[s, n], rs_rs.at[s, n])
            push(s, 4 + n, keep[s, n] + part_recv[s, n].astype(F32), step)

    def backward(e, hidden, act, slope):
        wait_gather(1, e)
        back = project(2, 1, e)
        d_gate = (back * slope).astype(BF16)
        d_up = (back * act).astype(BF16)
        rows = jnp.transpose(d_gate), jnp.transpose(d_up)
        push_far(e, 0, *rows)
        push_near(e, 0, *rows)
        push_far(e, 1, *rows)
        gg = jnp.sum(hidden.astype(F32) * back, axis=0, keepdims=True)
        gg_part[e] = jnp.broadcast_to(gg, (8, cap))
        for i in range(1, n_half):
            to_half(gg_part.at[e], gg_recv.at[e, i - 1], ggx_ss.at[e], ggx_rs.at[e], i).start()
        for q in range(2):
            part_own[2 * e + q] = row_block(e, q, 0, *rows)
        relay(e, 0)
        push_near(e, 1, *rows)
        return d_gate, d_up

    def weight_grads(e, hidden, d_gate, d_up):
        for h in range(n_half):
            for q in range(2):
                cols = pl.ds(h * quarter + q * fold, fold)
                x_h = rows_all[0, e, q, h]
                grads_g[e, :, cols] = dot(d_gate, x_h).astype(BF16)
                grads_u[e, :, cols] = dot(d_up, x_h).astype(BF16)
                grads_d[e, :, cols] = dot(hidden, rows_all[1, e, q, h]).astype(BF16)

    def send_home(e, q):
        s = 2 * e + q
        for n in (2, 3, 4, 5):
            wait_for(part_recv.at[s, n], rs_rs.at[s, n])
        low = part_own[s, low_rows] + part_recv[s, 4].astype(F32) + part_recv[s, 3].astype(F32)
        high = part_own[s, high_rows] + part_recv[s, 2].astype(F32) + part_recv[s, 5].astype(F32)
        total = jnp.concatenate([low.astype(BF16), high.astype(BF16)], axis=0)
        ret_send[s] = folded(dot(spread[e], total))
        ret_recv[s, me] = ret_send[s, me]
        send_all(ret_send.at[s], ret_recv.at[s], ret_ss.at[s], ret_rs.at[s])

    def gate_home():
        total = jnp.zeros((n_src, 128), F32)
        for e in range(2):
            wait_for(gg_recv.at[e], ggx_rs.at[e])
            gg = gg_part[e]
            for i in range(n_half - 1):
                gg = gg + gg_recv[e, i]
            top = gg.astype(BF16).astype(F32)
            mid_part = (gg - top).astype(BF16).astype(F32)
            rest = gg - top - mid_part
            sub = iota((8, cap), 0)
            split = jnp.where(sub == 0, top, jnp.where(sub == 1, mid_part, jnp.where(sub == 2, rest, 0.0)))
            row = jnp.sum(dot(split.astype(BF16), pack[e, 0]), axis=0, keepdims=True)
            own = iota((n_src, slots), 1) // 16 == iota((n_src, slots), 0)
            spread_row = jnp.where(own, jnp.broadcast_to(row, (n_src, slots)), 0.0)
            col = iota((slots, 128), 0)
            to_lane = ((col // 8) % 2 == 0) & (iota((slots, 128), 1) == e * 8 + col % 8)
            total = total + dot(spread_row, to_lane.astype(F32), precision=lax.Precision.HIGHEST)
        ggh_send[...] = total.reshape(n_src, 1, 128)
        ggh_recv[me] = ggh_send[me]
        send_all(ggh_send, ggh_recv, ggh_ss, ggh_rs)

    wait_all(cnt_recv, cnt_rs)
    make_pack(0)
    take_in(*PIECES[0])
    for load in loads:
        load.wait()
    make_home(0)
    take_in(*PIECES[1])
    make_home(1)
    take_in(*PIECES[2])
    fwd0 = forward(0)
    make_pack(1)
    take_in(*PIECES[3])
    make_spread(0)
    take_in(*PIECES[4])
    back0 = backward(0, *fwd0)
    relay(0, 1)
    take_in(*PIECES[5])
    make_spread(1)
    weight_grads(0, fwd0[0], *back0)
    take_in(*PIECES[6])
    fwd1 = forward(1)
    take_in(*PIECES[7])
    send_home(0, 0)
    send_home(0, 1)
    back1 = backward(1, *fwd1)
    relay(1, 1)
    gate_home()
    send_home(1, 0)
    send_home(1, 1)
    weight_grads(1, fwd1[0], *back1)

    wait_all(ggh_recv, ggh_rs)
    got = ggh_recv[...].reshape(n_src, 128)
    gg_rows = jnp.zeros((most, experts), F32)
    for e in range(2):
        lanes = (iota((most, 128), 1) == e * 8 + iota((most, 128), 0)).astype(F32)
        place = (iota((n_src, experts), 1) == 2 * iota((n_src, experts), 0) + e).astype(F32)
        picked = dot(lanes, got, NT, precision=lax.Precision.HIGHEST)
        gg_rows = gg_rows + dot(picked, place, precision=lax.Precision.HIGHEST)
    gg_out[...] = jnp.where(live, gg_rows / gates[...].astype(F32), 0.0).astype(BF16)

    wait_all(cnt_send, cnt_ss)
    wait_all(ggh_send, ggh_ss)
    for k, (a, e, q) in enumerate(PIECES):
        wait_all(fwd_send.at[k], fwd_ss.at[k])
        for n in range(6):
            wait_for(rows_all.at[a, e, q, 0, low_rows], ag_ss.at[k, n])
    for s in range(4):
        for n in range(6):
            wait_for(part_send.at[s, n], rs_ss.at[s, n])
    for e in range(2):
        wait_for(gg_recv.at[e], ggx_ss.at[e])

    def home_sum(s):
        wait_all(ret_recv.at[s], ret_rs.at[s])
        got = ret_recv[s].reshape(slots, lane)
        return [dot(home_g[s // 2, g], got) for g in range(2)]

    first = [home_sum(0), home_sum(1)]
    for q in range(2):
        last = home_sum(2 + q)
        for g in range(2):
            gt_out[:, pl.ds(q * fold + g * lane, lane)] = (first[q][g] + last[g]).astype(BF16)

    for s in range(4):
        wait_all(ret_send.at[s], ret_ss.at[s])


def write_out(a, b, c, d, e, ao, bo, co, do, eo, sem):
    copies = [
        pltpu.make_async_copy(src, dst, sem.at[k])
        for k, (src, dst) in enumerate(((b, bo), (c, co), (d, do), (a, ao), (e, eo)))
    ]
    for copy in copies:
        copy.start()
    for copy in copies:
        copy.wait()


def body(n_src, n_half, tokens, out_grad, w_gate, w_up, w_down, chosen_rows, counts, gate_values):
    tok_dev, quarter = tokens.shape
    experts, _, most = chosen_rows.shape
    per, hid, width = w_gate.shape
    cap = 4 * n_src
    fold = quarter // 2
    lane = fold // 2
    slots = n_src * 16
    vmem = pl.BlockSpec(memory_space=pltpu.VMEM)
    hbm = pl.BlockSpec(memory_space=pltpu.HBM)
    dma = pltpu.SemaphoreType.DMA
    grad_w = jax.ShapeDtypeStruct(w_gate.shape, BF16)
    shapes = (
        jax.ShapeDtypeStruct(tokens.shape, BF16),
        grad_w, grad_w, grad_w,
        jax.ShapeDtypeStruct((most, experts), BF16),
    )
    args = (
        tokens, out_grad,
        chosen_rows.reshape(experts, most).T, counts.T, gate_values.reshape(experts, most).T,
        w_gate, w_up, w_down,
    )
    outs = pl.pallas_call(
        functools.partial(kernel, n_src, n_half),
        out_shape=tuple(pltpu.VMEM(s.shape, s.dtype) for s in shapes),
        in_specs=[hbm] * 8,
        out_specs=(vmem,) * 5,
        scratch_shapes=[
            pltpu.VMEM(tokens.shape, BF16),
            pltpu.VMEM(tokens.shape, BF16),
            pltpu.VMEM((most, experts), jnp.int32),
            pltpu.VMEM((1, experts), jnp.int32),
            pltpu.VMEM((most, experts), BF16),
            dma((5,)),
            pltpu.VMEM((3, per, hid, width), BF16),
            dma((3,)),
            pltpu.VMEM((slots, tok_dev), BF16),
            pltpu.VMEM((n_src, 1, 128), F32),
            pltpu.VMEM((n_src, 1, 128), F32),
            pltpu.VMEM((8, n_src, 16, lane), BF16),
            pltpu.VMEM((8, n_src, 16, lane), BF16),
            pltpu.VMEM((2, 2, tok_dev, slots), BF16),
            pltpu.VMEM((2, 2, cap, slots), BF16),
            pltpu.VMEM((2, slots, cap), BF16),
            pltpu.VMEM((2, 2, 2, n_half, cap, fold), BF16),
            pltpu.VMEM((4, 6, cap // 2, fold), BF16),
            pltpu.VMEM((4, 6, cap // 2, fold), BF16),
            pltpu.VMEM((4, cap, fold), F32),
            pltpu.VMEM((4, 2, cap // 2, fold), F32),
            pltpu.VMEM((2, 8, cap), F32),
            pltpu.VMEM((2, n_half - 1, 8, cap), F32),
            pltpu.VMEM((n_src, 1, 128), F32),
            pltpu.VMEM((n_src, 1, 128), F32),
            pltpu.VMEM((4, n_src, 16, lane), BF16),
            pltpu.VMEM((4, n_src, 16, lane), BF16),
            dma, dma, dma((8,)), dma((8,)), dma((8, 6)), dma((8, 6)), dma((4, 6)), dma((4, 6)),
            dma((2,)), dma((2,)), dma((4,)), dma((4,)), dma, dma,
        ],
        compiler_params=pltpu.CompilerParams(
            collective_id=0, has_side_effects=True, vmem_limit_bytes=46 * 2**20
        ),
        cost_estimate=pl.CostEstimate(flops=4 * 10**9, bytes_accessed=10**7, transcendentals=10**5),
        name="experts_backward",
    )(*(pltpu.with_memory_space_constraint(a, pltpu.HBM) for a in args))
    outs = pl.pallas_call(
        write_out,
        out_shape=shapes,
        in_specs=[pl.BlockSpec(memory_space=pl.ANY)] * 5,
        out_specs=(hbm,) * 5,
        scratch_shapes=[dma((5,))],
        compiler_params=pltpu.CompilerParams(vmem_limit_bytes=2**20),
        name="write_out",
    )(*outs)
    return outs[:4] + (outs[4].T.reshape(experts, 1, most),)


def solution(mesh):
    return jax.shard_map(
        functools.partial(body, mesh.shape["expert"], mesh.shape["half"]),
        mesh=mesh,
        in_specs=(
            P("expert", "half"),
            P("expert", "half"),
            P("expert", "half", None),
            P("expert", "half", None),
            P("expert", "half", None),
            P(None, "expert", None),
            P(None, "expert"),
            P(None, "expert", None),
        ),
        out_specs=(
            P("expert", "half"),
            P("expert", "half", None),
            P("expert", "half", None),
            P("expert", "half", None),
            P(None, "expert", None),
        ),
        check_vma=False,
    )
```

```python
import functools

import jax
import jax.numpy as jnp
from jax import lax
from jax.experimental import pallas as pl
from jax.experimental.pallas import tpu as pltpu
from jax.sharding import PartitionSpec as P

MESH = pl.DeviceIdType.MESH
F32, BF16 = jnp.float32, jnp.bfloat16
NT = ((1,), (1,))
PIECES = tuple((a, e, q) for e in range(2) for a in range(2) for q in range(2))


def iota(shape, dim):
    return lax.broadcasted_iota(jnp.int32, shape, dim)


def dot(a, b, dims=((1,), (0,)), precision=None):
    return lax.dot_general(a, b, (dims, ((), ())), preferred_element_type=F32, precision=precision)


def kernel(
    n_src, n_half,
    tok_hbm, out_grad_hbm, chosen_hbm, counts_hbm, gates_hbm, wg_hbm, wu_hbm, wd_hbm,
    gt_out, grads_g, grads_u, grads_d, gg_out,
    tok, out_grad, chosen, counts, gates, in_sem,
    w_buf, w_sem, hot_buf,
    cnt_send, cnt_recv, fwd_send, fwd_recv,
    home_g, pack, spread,
    rows_all, part_send, part_recv, part_own, keep,
    gg_part, gg_recv, ggh_send, ggh_recv,
    ret_send, ret_recv,
    cnt_ss, cnt_rs, fwd_ss, fwd_rs, ag_ss, ag_rs, rs_ss, rs_rs,
    ggx_ss, ggx_rs, ret_ss, ret_rs, ggh_ss, ggh_rs,
):
    me = lax.axis_index("expert")
    half = lax.axis_index("half")
    tokens = tok.shape[0]
    quarter = tok.shape[1]
    fold = quarter // 2
    lane = fold // 2
    slots = n_src * 16
    cap = rows_all.shape[4]
    mid = cap // 2
    hid = wg_hbm.shape[1]
    most, experts = chosen.shape
    piece_of = {piece: k for k, piece in enumerate(PIECES)}

    ins = [
        pltpu.make_async_copy(src, dst, in_sem.at[k])
        for k, (src, dst) in enumerate((
            (chosen_hbm, chosen), (counts_hbm, counts), (gates_hbm, gates), (tok_hbm, tok), (out_grad_hbm, out_grad)
        ))
    ]
    loads = [
        pltpu.make_async_copy(ref, w_buf.at[k], w_sem.at[k]) for k, ref in enumerate((wg_hbm, wu_hbm, wd_hbm))
    ]
    for copy in ins:
        copy.start()

    barrier = pltpu.get_barrier_semaphore()

    for start, stop in ((n_src // 2, n_src), (1, n_src // 2)):
        @pl.loop(start, stop)
        def _(i):
            pl.semaphore_signal(barrier, inc=1, device_id={"expert": lax.rem(me + i, n_src)}, device_id_type=MESH)

    for i in range(1, n_half):
        pl.semaphore_signal(barrier, inc=1, device_id={"half": lax.rem(half + i, n_half)}, device_id_type=MESH)

    for copy in ins:
        copy.wait()
    for load in loads:
        load.start()

    live = iota((most, experts), 0) < counts[...]
    chosen_live = jnp.where(live, chosen[...], -1).astype(F32).astype(BF16)
    gates_live = jnp.where(live, gates[...].astype(F32), 0.0).astype(BF16)

    def send_all(src, dst, ss, rs):
        @pl.loop(1, n_src)
        def _(i):
            to = lax.rem(me + i, n_src)
            pltpu.make_async_remote_copy(
                src_ref=src.at[to], dst_ref=dst.at[me], send_sem=ss, recv_sem=rs,
                device_id={"expert": to}, device_id_type=MESH,
            ).start()

    def wait_for(buf, sem):
        pltpu.make_async_copy(buf, buf, sem).wait()

    def wait_all(buf, sem):
        wait_for(buf.at[pl.ds(0, n_src - 1)], sem)

    def folded(wide):
        low = (iota((slots, lane), 0) // 8) % 2 == 0
        return jnp.where(low, wide[:, :lane], wide[:, lane:]).astype(BF16).reshape(n_src, 16, lane)

    def spread_column(e, table):
        mine = (iota((slots, experts), 1) == 2 * (iota((slots, experts), 0) // 16) + e).astype(BF16)
        slot_j = iota((slots, most), 1) == iota((slots, most), 0) % 8
        picked = jnp.where(slot_j, dot(mine, table, NT), 0.0).astype(BF16)
        return dot(picked, jnp.ones((most, tokens), BF16))

    def pick(a, e):
        hot = spread_column(e, chosen_live) == iota((slots, tokens), 1).astype(F32)
        value = 1.0 if a == 0 else spread_column(e, gates_live)
        hot_buf[...] = jnp.where(hot, value, 0.0).astype(BF16)

    def fill(a, e, q):
        k = piece_of[a, e, q]
        src = tok if a == 0 else out_grad
        fwd_send[k] = folded(dot(hot_buf[...], src[:, pl.ds(q * fold, fold)]))
        fwd_recv[k, me] = fwd_send[k, me]

    def send_piece(k):
        send_all(fwd_send.at[k], fwd_recv.at[k], fwd_ss.at[k], fwd_rs.at[k])

    ahead = 3

    def prep(k):
        if k >= len(PIECES):
            return
        a, e, q = PIECES[k]
        if q == 0:
            pick(a, e)
        fill(a, e, q)

    prep(0)
    pl.semaphore_wait(barrier, n_src - 1 + n_half - 1)
    send_piece(0)
    count_wide = jnp.broadcast_to(counts[...].astype(F32), (128, experts)).astype(BF16)
    rows_to = jnp.zeros((n_src, 128), F32)
    for e in range(2):
        mine = (iota((n_src, experts), 1) == 2 * iota((n_src, experts), 0) + e).astype(BF16)
        rows_to = rows_to + jnp.where(iota((n_src, 128), 1) == e, dot(mine, count_wide, NT), 0.0)
    cnt_send[...] = rows_to.reshape(n_src, 1, 128)
    cnt_recv[me] = cnt_send[me]
    send_all(cnt_send, cnt_recv, cnt_ss, cnt_rs)
    for k in range(1, ahead):
        prep(k)
        send_piece(k)
    prep(ahead)

    def make_pack(e):
        count_all = cnt_recv[...].reshape(n_src, 128).astype(BF16)
        by_col = dot(count_all, (iota((128, slots), 0) == e).astype(BF16))
        src_of = iota((n_src, slots), 1) // 16
        before = jnp.sum(jnp.where(iota((n_src, slots), 0) < src_of, by_col, 0.0), axis=0, keepdims=True)
        size = jnp.sum(jnp.where(iota((n_src, slots), 0) == src_of, by_col, 0.0), axis=0, keepdims=True)
        j = (iota((1, slots), 1) % 8).astype(F32)
        place = jnp.where(j < size, before + j, -1.0)
        hit = place == iota((cap, slots), 0).astype(F32)
        in_half = (iota((cap, slots), 1) // 8) % 2
        for g in range(2):
            pack[e, g] = jnp.where(hit & (in_half == g), 1.0, 0.0).astype(BF16)

    def make_spread(e):
        count_all = cnt_recv[...].reshape(n_src, 128).astype(BF16)
        own_wide = dot(count_all, (iota((128, cap), 0) == e).astype(BF16)).astype(BF16)
        src_row = iota((slots, n_src), 0) // 16
        before = dot((iota((slots, n_src), 1) < src_row).astype(BF16), own_wide)
        size = dot((iota((slots, n_src), 1) == src_row).astype(BF16), own_wide)
        j = (iota((slots, cap), 0) % 8).astype(F32)
        place = jnp.where(j < size, before + j, -1.0)
        spread[e] = jnp.where(place == iota((slots, cap), 1).astype(F32), 1.0, 0.0).astype(BF16)

    def make_home(e):
        in_half = (iota((tokens, slots), 1) // 8) % 2
        mine = (iota((experts, slots), 0) == 2 * (iota((experts, slots), 1) // 16) + e).astype(BF16)
        row = dot(chosen_live, mine)
        row = jnp.sum(jnp.where(iota((most, slots), 0) == iota((most, slots), 1) % 8, row, 0.0), axis=0, keepdims=True)
        hit = row == iota((tokens, slots), 0).astype(F32)
        for g in range(2):
            home_g[e, g] = jnp.where(hit & (in_half == g), 1.0, 0.0).astype(BF16)

    def to_half(src, dst, ss, rs, step):
        return pltpu.make_async_remote_copy(
            src_ref=src, dst_ref=dst, send_sem=ss, recv_sem=rs,
            device_id={"half": lax.rem(half + step, n_half)}, device_id_type=MESH,
        )

    low_rows, high_rows = pl.ds(0, mid), pl.ds(mid, mid)

    def pass_on(k, ref, n, step):
        to_half(ref, ref, ag_ss.at[k, n], ag_rs.at[k, n], step).start()

    def take_in(a, e, q):
        k = piece_of[a, e, q]
        wait_all(fwd_recv.at[k], fwd_rs.at[k])
        got = fwd_recv[k].reshape(slots, lane)
        for g in range(2):
            rows_all[a, e, q, half, :, pl.ds(g * lane, lane)] = dot(pack[e, g], got).astype(BF16)
        mine = rows_all.at[a, e, q, half]
        pass_on(k, mine.at[low_rows], 0, 1)
        pass_on(k, mine.at[high_rows], 1, 3)
        pass_on(k, mine.at[high_rows], 2, 1)
        pass_on(k, mine.at[low_rows], 3, 3)
        if k + ahead < len(PIECES):
            send_piece(k + ahead)
            prep(k + ahead + 1)
    def hand_on(a, e, q):
        k = piece_of[a, e, q]
        left = rows_all.at[a, e, q, lax.rem(half + 3, n_half), low_rows]
        right = rows_all.at[a, e, q, lax.rem(half + 1, n_half), high_rows]
        wait_for(left, ag_rs.at[k, 0])
        pass_on(k, left, 4, 1)
        wait_for(right, ag_rs.at[k, 1])
        pass_on(k, right, 5, 3)

    def wait_gather(a, e):
        for q in range(2):
            for n in (2, 3, 4, 5):
                wait_for(rows_all.at[a, e, q, 0, low_rows], ag_rs.at[piece_of[a, e, q], n])

    def project(w, a, e):
        total = jnp.zeros((hid, cap), F32)
        for h in range(n_half):
            for q in range(2):
                cols = pl.ds(h * quarter + q * fold, fold)
                total = total + dot(w_buf[w, e, :, cols], rows_all[a, e, q, h], NT)
        return total

    def forward(e):
        wait_gather(0, e)
        pre_gate = project(0, 0, e)
        pre_up = project(1, 0, e)
        sig = 1.0 / (1.0 + jnp.exp(-pre_gate))
        act = pre_gate * sig
        hidden = (act * pre_up).astype(BF16)
        slope = pre_up * sig * (1.0 + pre_gate * (1.0 - sig))
        return hidden, act, slope

    def row_block(e, q, step, dg_r, du_r):
        to = lax.rem(half + step, n_half)
        cols = pl.ds(pl.multiple_of(to * quarter + q * fold, fold), fold)
        return dot(dg_r, w_buf[0, e, :, cols]) + dot(du_r, w_buf[1, e, :, cols])

    def push(s, n, block, step):
        part_send[s, n] = block.astype(BF16)
        to_half(part_send.at[s, n], part_recv.at[s, n], rs_ss.at[s, n], rs_rs.at[s, n], step).start()

    def push_far(e, q, *rows):
        s = 2 * e + q
        far = row_block(e, q, 2, *rows)
        push(s, 0, far[:mid], 1)
        push(s, 1, far[mid:], 3)

    def push_near(e, q, *rows):
        s = 2 * e + q
        right = row_block(e, q, 1, *rows)
        push(s, 2, right[mid:], 1)
        keep[s, 0] = right[:mid]
        left = row_block(e, q, 3, *rows)
        push(s, 3, left[:mid], 3)
        keep[s, 1] = left[mid:]

    def relay(e, q):
        s = 2 * e + q
        for n, step in ((0, 1), (1, 3)):
            wait_for(part_recv.at[s, n], rs_rs.at[s, n])
            push(s, 4 + n, keep[s, n] + part_recv[s, n].astype(F32), step)

    def backward(e, hidden, act, slope):
        wait_gather(1, e)
        back = project(2, 1, e)
        d_gate = (back * slope).astype(BF16)
        d_up = (back * act).astype(BF16)
        rows = jnp.transpose(d_gate), jnp.transpose(d_up)
        push_far(e, 0, *rows)
        push_near(e, 0, *rows)
        push_far(e, 1, *rows)
        gg = jnp.sum(hidden.astype(F32) * back, axis=0, keepdims=True)
        gg_part[e] = jnp.broadcast_to(gg, (8, cap))
        for i in range(1, n_half):
            to_half(gg_part.at[e], gg_recv.at[e, i - 1], ggx_ss.at[e], ggx_rs.at[e], i).start()
        for q in range(2):
            part_own[2 * e + q] = row_block(e, q, 0, *rows)
        return d_gate, d_up, rows

    def reduce_rest(e, rows):
        relay(e, 0)
        push_near(e, 1, *rows)
        relay(e, 1)

    def weight_grads(e, hidden, d_gate, d_up):
        for h in range(n_half):
            for q in range(2):
                cols = pl.ds(h * quarter + q * fold, fold)
                x_h = rows_all[0, e, q, h]
                grads_g[e, :, cols] = dot(d_gate, x_h).astype(BF16)
                grads_u[e, :, cols] = dot(d_up, x_h).astype(BF16)
                grads_d[e, :, cols] = dot(hidden, rows_all[1, e, q, h]).astype(BF16)

    def send_home(e, q):
        s = 2 * e + q
        for n in (2, 3, 4, 5):
            wait_for(part_recv.at[s, n], rs_rs.at[s, n])
        low = part_own[s, low_rows] + part_recv[s, 4].astype(F32) + part_recv[s, 3].astype(F32)
        high = part_own[s, high_rows] + part_recv[s, 2].astype(F32) + part_recv[s, 5].astype(F32)
        total = jnp.concatenate([low.astype(BF16), high.astype(BF16)], axis=0)
        ret_send[s] = folded(dot(spread[e], total))
        ret_recv[s, me] = ret_send[s, me]
        send_all(ret_send.at[s], ret_recv.at[s], ret_ss.at[s], ret_rs.at[s])

    def gate_home():
        total = jnp.zeros((n_src, 128), F32)
        for e in range(2):
            wait_for(gg_recv.at[e], ggx_rs.at[e])
            gg = gg_part[e]
            for i in range(n_half - 1):
                gg = gg + gg_recv[e, i]
            top = gg.astype(BF16).astype(F32)
            mid_part = (gg - top).astype(BF16).astype(F32)
            rest = gg - top - mid_part
            sub = iota((8, cap), 0)
            split = jnp.where(sub == 0, top, jnp.where(sub == 1, mid_part, jnp.where(sub == 2, rest, 0.0)))
            row = jnp.sum(dot(split.astype(BF16), pack[e, 0]), axis=0, keepdims=True)
            own = iota((n_src, slots), 1) // 16 == iota((n_src, slots), 0)
            spread_row = jnp.where(own, jnp.broadcast_to(row, (n_src, slots)), 0.0)
            col = iota((slots, 128), 0)
            to_lane = ((col // 8) % 2 == 0) & (iota((slots, 128), 1) == e * 8 + col % 8)
            total = total + dot(spread_row, to_lane.astype(F32), precision=lax.Precision.HIGHEST)
        ggh_send[...] = total.reshape(n_src, 1, 128)
        ggh_recv[me] = ggh_send[me]
        send_all(ggh_send, ggh_recv, ggh_ss, ggh_rs)

    wait_all(cnt_recv, cnt_rs)
    make_pack(0)
    take_in(*PIECES[0])
    for load in loads:
        load.wait()
    hand_on(*PIECES[0])
    make_home(0)
    take_in(*PIECES[1])
    hand_on(*PIECES[1])
    make_home(1)
    take_in(*PIECES[2])
    hand_on(*PIECES[2])
    fwd0 = forward(0)
    make_pack(1)
    take_in(*PIECES[3])
    hand_on(*PIECES[3])
    make_spread(0)
    take_in(*PIECES[4])
    *back0, rows0 = backward(0, *fwd0)
    hand_on(*PIECES[4])
    reduce_rest(0, rows0)
    take_in(*PIECES[5])
    make_spread(1)
    hand_on(*PIECES[5])
    weight_grads(0, fwd0[0], *back0)
    take_in(*PIECES[6])
    send_home(0, 0)
    hand_on(*PIECES[6])
    fwd1 = forward(1)
    take_in(*PIECES[7])
    send_home(0, 1)
    hand_on(*PIECES[7])
    *back1, rows1 = backward(1, *fwd1)
    reduce_rest(1, rows1)
    send_home(1, 0)
    gate_home()
    send_home(1, 1)
    weight_grads(1, fwd1[0], *back1)

    wait_all(ggh_recv, ggh_rs)
    got = ggh_recv[...].reshape(n_src, 128)
    gg_rows = jnp.zeros((most, experts), F32)
    for e in range(2):
        lanes = (iota((most, 128), 1) == e * 8 + iota((most, 128), 0)).astype(F32)
        place = (iota((n_src, experts), 1) == 2 * iota((n_src, experts), 0) + e).astype(F32)
        picked = dot(lanes, got, NT, precision=lax.Precision.HIGHEST)
        gg_rows = gg_rows + dot(picked, place, precision=lax.Precision.HIGHEST)
    gg_out[...] = jnp.where(live, gg_rows / gates[...].astype(F32), 0.0).astype(BF16)

    wait_all(cnt_send, cnt_ss)
    wait_all(ggh_send, ggh_ss)
    for k, (a, e, q) in enumerate(PIECES):
        wait_all(fwd_send.at[k], fwd_ss.at[k])
        for n in range(6):
            wait_for(rows_all.at[a, e, q, 0, low_rows], ag_ss.at[k, n])
    for s in range(4):
        for n in range(6):
            wait_for(part_send.at[s, n], rs_ss.at[s, n])
    for e in range(2):
        wait_for(gg_recv.at[e], ggx_ss.at[e])

    def home_sum(s):
        wait_all(ret_recv.at[s], ret_rs.at[s])
        got = ret_recv[s].reshape(slots, lane)
        return [dot(home_g[s // 2, g], got) for g in range(2)]

    first = [home_sum(0), home_sum(1)]
    for q in range(2):
        last = home_sum(2 + q)
        for g in range(2):
            gt_out[:, pl.ds(q * fold + g * lane, lane)] = (first[q][g] + last[g]).astype(BF16)

    for s in range(4):
        wait_all(ret_send.at[s], ret_ss.at[s])


def write_out(a, b, c, d, e, ao, bo, co, do, eo, sem):
    copies = [
        pltpu.make_async_copy(src, dst, sem.at[k])
        for k, (src, dst) in enumerate(((b, bo), (c, co), (d, do), (a, ao), (e, eo)))
    ]
    for copy in copies:
        copy.start()
    for copy in copies:
        copy.wait()


def body(n_src, n_half, tokens, out_grad, w_gate, w_up, w_down, chosen_rows, counts, gate_values):
    tok_dev, quarter = tokens.shape
    experts, _, most = chosen_rows.shape
    per, hid, width = w_gate.shape
    cap = 4 * n_src
    fold = quarter // 2
    lane = fold // 2
    slots = n_src * 16
    vmem = pl.BlockSpec(memory_space=pltpu.VMEM)
    hbm = pl.BlockSpec(memory_space=pltpu.HBM)
    dma = pltpu.SemaphoreType.DMA
    grad_w = jax.ShapeDtypeStruct(w_gate.shape, BF16)
    shapes = (
        jax.ShapeDtypeStruct(tokens.shape, BF16),
        grad_w, grad_w, grad_w,
        jax.ShapeDtypeStruct((most, experts), BF16),
    )
    args = (
        tokens, out_grad,
        chosen_rows.reshape(experts, most).T, counts.T, gate_values.reshape(experts, most).T,
        w_gate, w_up, w_down,
    )
    outs = pl.pallas_call(
        functools.partial(kernel, n_src, n_half),
        out_shape=tuple(pltpu.VMEM(s.shape, s.dtype) for s in shapes),
        in_specs=[hbm] * 8,
        out_specs=(vmem,) * 5,
        scratch_shapes=[
            pltpu.VMEM(tokens.shape, BF16),
            pltpu.VMEM(tokens.shape, BF16),
            pltpu.VMEM((most, experts), jnp.int32),
            pltpu.VMEM((1, experts), jnp.int32),
            pltpu.VMEM((most, experts), BF16),
            dma((5,)),
            pltpu.VMEM((3, per, hid, width), BF16),
            dma((3,)),
            pltpu.VMEM((slots, tok_dev), BF16),
            pltpu.VMEM((n_src, 1, 128), F32),
            pltpu.VMEM((n_src, 1, 128), F32),
            pltpu.VMEM((8, n_src, 16, lane), BF16),
            pltpu.VMEM((8, n_src, 16, lane), BF16),
            pltpu.VMEM((2, 2, tok_dev, slots), BF16),
            pltpu.VMEM((2, 2, cap, slots), BF16),
            pltpu.VMEM((2, slots, cap), BF16),
            pltpu.VMEM((2, 2, 2, n_half, cap, fold), BF16),
            pltpu.VMEM((4, 6, cap // 2, fold), BF16),
            pltpu.VMEM((4, 6, cap // 2, fold), BF16),
            pltpu.VMEM((4, cap, fold), F32),
            pltpu.VMEM((4, 2, cap // 2, fold), F32),
            pltpu.VMEM((2, 8, cap), F32),
            pltpu.VMEM((2, n_half - 1, 8, cap), F32),
            pltpu.VMEM((n_src, 1, 128), F32),
            pltpu.VMEM((n_src, 1, 128), F32),
            pltpu.VMEM((4, n_src, 16, lane), BF16),
            pltpu.VMEM((4, n_src, 16, lane), BF16),
            dma, dma, dma((8,)), dma((8,)), dma((8, 6)), dma((8, 6)), dma((4, 6)), dma((4, 6)),
            dma((2,)), dma((2,)), dma((4,)), dma((4,)), dma, dma,
        ],
        compiler_params=pltpu.CompilerParams(
            collective_id=0, has_side_effects=True, vmem_limit_bytes=46 * 2**20
        ),
        cost_estimate=pl.CostEstimate(flops=4 * 10**9, bytes_accessed=10**7, transcendentals=10**5),
        name="experts_backward",
    )(*(pltpu.with_memory_space_constraint(a, pltpu.HBM) for a in args))
    outs = pl.pallas_call(
        write_out,
        out_shape=shapes,
        in_specs=[pl.BlockSpec(memory_space=pl.ANY)] * 5,
        out_specs=(hbm,) * 5,
        scratch_shapes=[dma((5,))],
        compiler_params=pltpu.CompilerParams(vmem_limit_bytes=2**20),
        name="write_out",
    )(*outs)
    return outs[:4] + (outs[4].T.reshape(experts, 1, most),)


def solution(mesh):
    return jax.shard_map(
        functools.partial(body, mesh.shape["expert"], mesh.shape["half"]),
        mesh=mesh,
        in_specs=(
            P("expert", "half"),
            P("expert", "half"),
            P("expert", "half", None),
            P("expert", "half", None),
            P("expert", "half", None),
            P(None, "expert", None),
            P(None, "expert"),
            P(None, "expert", None),
        ),
        out_specs=(
            P("expert", "half"),
            P("expert", "half", None),
            P("expert", "half", None),
            P("expert", "half", None),
            P(None, "expert", None),
        ),
        check_vma=False,
    )
```
